512 devices in a mesh: row: 8 (over z_lo, x), col: 8 (over z_hi, core), depth: 8 (over y).
Axes of the slice: x: 4, y: 8, z: 8 (z_hi: 4, z_lo: 2; z = z_hi * 2 + z_lo), core: 2. Of those that a mesh axis runs over, the one named last changes fastest.
Arguments:
- stream: bfloat16 [256, 8192], P(('row', 'depth'), 'col'), may hold values from -6 to 6
- norm_gain: float32 [8192], P('col'), may hold values from 0.5 to 1.5
- w_gate: bfloat16 [8192, 21504], P('col', ('row', 'depth')), may hold values from -0.0625 to 0.0625
- w_up: bfloat16 [8192, 21504], P('col', ('row', 'depth')), may hold values from -0.0625 to 0.0625
- w_down: bfloat16 [21504, 8192], P(('row', 'depth'), 'col'), may hold values from -0.0390625 to 0.0390625
- d_mixed: bfloat16 [256, 8192], P(('row', 'depth'), 'col'), may hold values from -6 to 6
Outputs:
- new_stream: bfloat16 [256, 8192], P(('row', 'depth'), 'col')
- grad_stream: bfloat16 [256, 8192], P(('row', 'depth'), 'col')
- grad_gate: bfloat16 [8192, 21504], P('col', ('row', 'depth'))
- grad_up: bfloat16 [8192, 21504], P('col', ('row', 'depth'))
- grad_down: bfloat16 [21504, 8192], P(('row', 'depth'), 'col')
The draws below stay inside these ranges and needn't reach their ends.
All inputs are finite; a program needn't handle non-finite values.
Results may differ from the reference program's by a relative error of at most 0.0067.
Values may be sent and summed in bfloat16 or wider, within the bound.
A program may use at most 64 MiB of HBM per device.

```python
import jax
import jax.numpy as jnp
from jax import lax

D = 8192
FF = 21504
TOKENS = 256


def block_scale(stream_key, dims, split, least, high):
    level, own = 1.0, jax.random.fold_in(stream_key, 6)
    for position, blocks in split:
        heights = jnp.exp(jax.random.uniform(jax.random.fold_in(own, position), (blocks,), jnp.float32, least / len(split), high / len(split)))
        level = level * jnp.repeat(heights, dims[position] // blocks).reshape([-1 if axis == position else 1 for axis in range(len(dims))])
    return level


def noise(key, dims, scale, limit, cuts=(), kind=jnp.bfloat16):
    array = scale * jax.random.normal(key, dims, jnp.float32)
    if cuts:
        array = array * block_scale(key, dims, cuts, -0.22, 0.18)
    return jnp.clip(array, -limit, limit).astype(kind)


def setup_inputs(seed: int = 0) -> dict:
    key_list = jax.random.split(jax.random.key(seed), 7)
    stream = noise(key_list[0], (TOKENS, D), 1.0, 6.0, ((0, 64), (1, 8)))
    norm_gain = jnp.clip(1.0 + 0.1 * jax.random.normal(key_list[1], (D,), jnp.float32), 0.5, 1.5)
    w_gate = noise(key_list[2], (D, FF), D ** -0.5, 0.0625, ((0, 8), (1, 64)))
    w_up = noise(key_list[3], (D, FF), D ** -0.5, 0.0625, ((0, 8), (1, 64)))
    w_down = noise(key_list[4], (FF, D), FF ** -0.5, 0.0390625, ((0, 64), (1, 8)))
    d_mixed = noise(key_list[5], (TOKENS, D), 1.0, 6.0, ((0, 64), (1, 8)))
    return {"stream": stream, "norm_gain": norm_gain, "w_gate": w_gate, "w_up": w_up, "w_down": w_down, "d_mixed": d_mixed}


epsilon = 1e-05

def reference(stream, norm_gain, w_gate, w_up, w_down, d_mixed):
    stream_f = stream.astype(jnp.float32)
    square_sum = lax.optimization_barrier(jnp.sum(stream_f * stream_f, axis=1, keepdims=True))
    inv_rms = lax.rsqrt(square_sum / D + epsilon)
    normed = (stream_f * inv_rms * norm_gain[None, :]).astype(jnp.bfloat16)
    gate = jnp.dot(normed, w_gate, preferred_element_type=jnp.float32)
    up_proj = jnp.dot(normed, w_up, preferred_element_type=jnp.float32)
    sigmoid_gate = jax.nn.sigmoid(gate)
    activated = gate * sigmoid_gate
    hidden = (activated * up_proj).astype(jnp.bfloat16)
    new_stream = (stream_f + jnp.dot(hidden, w_down, preferred_element_type=jnp.float32)).astype(jnp.bfloat16)
    grad_down = lax.dot_general(hidden, d_mixed, (((0,), (0,)), ((), ())), preferred_element_type=jnp.float32).astype(jnp.bfloat16)
    d_hidden = lax.dot_general(d_mixed, w_down, (((1,), (1,)), ((), ())), preferred_element_type=jnp.float32)
    d_gate = (d_hidden * up_proj * sigmoid_gate * (1.0 + gate * (1.0 - sigmoid_gate))).astype(jnp.bfloat16)
    d_up = (d_hidden * activated).astype(jnp.bfloat16)
    grad_gate = lax.dot_general(normed, d_gate, (((0,), (0,)), ((), ())), preferred_element_type=jnp.float32).astype(jnp.bfloat16)
    grad_up = lax.dot_general(normed, d_up, (((0,), (0,)), ((), ())), preferred_element_type=jnp.float32).astype(jnp.bfloat16)
    d_normed = lax.dot_general(d_gate, w_gate, (((1,), (1,)), ((), ())), preferred_element_type=jnp.float32)
    d_normed = d_normed + lax.dot_general(d_up, w_up, (((1,), (1,)), ((), ())), preferred_element_type=jnp.float32)
    d_scaled = d_normed * norm_gain[None, :]
    inner_sum = lax.optimization_barrier(jnp.sum(d_scaled * stream_f, axis=1, keepdims=True))
    d_stream = inv_rms * d_scaled - stream_f * inv_rms ** 3 * inner_sum / D
    grad_stream = (d_mixed.astype(jnp.float32) + d_stream).astype(jnp.bfloat16)
    return (new_stream, grad_stream, grad_gate, grad_up, grad_down)
```

```python
import functools

import jax
import jax.numpy as jnp
from jax import lax
from jax.experimental import pallas as pl
from jax.experimental.pallas import tpu as pltpu
from jax.sharding import PartitionSpec as P

F32, BF16 = jnp.float32, jnp.bfloat16
LANES = 128
EPSILON = 1e-05


def dot(a, b, dims=((1,), (0,))):
    return lax.dot_general(a, b, (dims, ((), ())), preferred_element_type=F32)


def kernel(
    sizes,
    stream_hbm, mixed_hbm, gain_hbm, wg_hbm, wu_hbm, wd_hbm,
    new_hbm, dstream_hbm, gg_hbm, gu_hbm, gd_hbm,
    stream_ref, mixed_ref, gain_ref, w_down, w_both,
    norm_parts, norm_all, mixed_parts, mixed_rows, mixed_all,
    partial, pair_out, pair_in, quad_out, quad_in,
    act_all, act_rows,
    out_send, out_recv, out_send2, out_recv2,
    dn_send, dn_recv, dn_send2, dn_recv2,
    new_out, dstream_out, gg_out, gu_out, gd_out,
    local_sem, send_sem, recv_sem,
):
    R, C, Y, fh, D = sizes
    mine, wide = stream_ref.shape
    fw = act_all.shape[2]
    low, high = fh // LANES * LANES, pl.cdiv(fh, LANES) * LANES
    spare = 3 * fh
    last = fw - LANES
    Z = C // 2
    tokens = R * Y * mine
    row, col, dep = (lax.axis_index(a) for a in ("row", "col", "depth"))
    zh, core = lax.div(col, 2), lax.rem(col, 2)
    sibling = zh * 2 + 1 - core

    barrier = pltpu.get_barrier_semaphore()
    for k in range(1, R):
        pl.semaphore_signal(barrier, 1, device_id={"row": lax.rem(row + k, R)})
    for k in range(1, Y):
        pl.semaphore_signal(barrier, 1, device_id={"depth": lax.rem(dep + k, Y)})
    for k in range(1, Z):
        pl.semaphore_signal(
            barrier, 1, device_id={"col": lax.rem(zh + k, Z) * 2 + core}
        )
    pl.semaphore_signal(barrier, 1, device_id={"col": sibling})

    loads = [
        pltpu.make_async_copy(a, b, local_sem.at[i])
        for i, (a, b) in enumerate([
            (stream_hbm, stream_ref),
            (gain_hbm, gain_ref),
            (mixed_hbm, mixed_ref),
            (wg_hbm, w_both.at[pl.ds(fh, fh)]),
            (wu_hbm, w_both.at[pl.ds(2 * fh, fh)]),
            (wd_hbm, w_down.at[pl.ds(0, fh)]),
        ])
    ]
    for copy in loads:
        copy.start()

    sent = []

    def send(src, dst, here, there, to):
        copy = pltpu.make_async_remote_copy(
            src_ref=src, dst_ref=dst,
            send_sem=send_sem.at[here], recv_sem=recv_sem.at[there], device_id=to,
        )
        copy.start()
        sent.append(copy)

    def receive(dst, slot, to):
        pltpu.make_async_remote_copy(
            src_ref=dst, dst_ref=dst,
            send_sem=send_sem.at[0], recv_sem=recv_sem.at[slot], device_id=to,
        ).wait_recv()

    def exchange(axis, base, source, target):
        me, n = (row, R) if axis == "row" else (dep, Y)
        others = [lax.rem(me + k, n) for k in range(1, n)]
        for k, p in enumerate(others):
            send(source(p), target(me), base + k, base + me, {axis: p})

        def finish():
            for p in others:
                receive(target(p), base + p, {axis: p})

        return finish

    base = iter(range(0, 96, 8))

    for copy in loads[:3]:
        copy.wait()
    stream = stream_ref[...].astype(F32)
    squares = jnp.sum(stream * stream, axis=1, keepdims=True)
    lane = lax.broadcasted_iota(jnp.int32, (mine, LANES), 1)
    norm_parts[row, :, 0:wide] = (stream * gain_ref[...]).astype(BF16)
    norm_parts[row, :, wide : wide + LANES] = jnp.where(
        lane == spare - last, squares, 0.0
    ).astype(BF16)
    mixed_parts[dep] = mixed_ref[...]

    pl.semaphore_wait(barrier, (R - 1) + (Y - 1) + (Z - 1) + 1)
    n1 = exchange("row", next(base), lambda p: norm_parts.at[row], lambda q: norm_parts.at[q])
    d1 = exchange("depth", next(base), lambda p: mixed_parts.at[dep], lambda q: mixed_parts.at[q])
    n1()
    norm_all[dep] = norm_parts[...].astype(F32).reshape(norm_all.shape[1:]).astype(BF16)
    n2 = exchange("depth", next(base), lambda p: norm_all.at[dep], lambda q: norm_all.at[q])
    d1()
    mixed_rows[row] = mixed_parts[...].astype(F32).reshape(mixed_rows.shape[1:]).astype(BF16)
    d2 = exchange("row", next(base), lambda p: mixed_rows.at[row], lambda q: mixed_rows.at[q])

    for copy in loads[3:]:
        copy.wait()
    w_down[fh:high, :] = jnp.zeros((high - fh, wide), BF16)
    w_both[low:fh, :] = jnp.zeros((fh - low, wide), BF16)
    w_both[spare:fw, :] = jnp.zeros((fw - spare, wide), BF16)
    t = lax.broadcasted_iota(jnp.int32, (tokens, tokens), 0)
    u = lax.broadcasted_iota(jnp.int32, (tokens, tokens), 1)
    by_row = ((t // mine) % R) * (Y * mine) + (t // (R * mine)) * mine + t % mine
    to_depth = (u == by_row).astype(F32).astype(BF16)
    by_depth = ((t // mine) % Y) * (R * mine) + (t // (Y * mine)) * mine + t % mine
    to_row = (u == by_depth).astype(F32).astype(BF16)

    n2()
    normed = norm_all[...].reshape(tokens, wide + LANES)
    both = dot(normed[:, 0:wide], w_both[low:fw, :], ((1,), (1,)))
    partial[:, :, low:fw] = both.reshape(Y, R * mine, fw - low)
    partial[:, :, last:fw] += norm_all[:, :, wide : wide + LANES].astype(F32)
    d2()
    mixed_all[...] = dot(to_depth, mixed_rows[...].reshape(tokens, wide)).astype(BF16)
    dh = dot(mixed_all[...], w_down[...], ((1,), (1,))).reshape(Y, R * mine, high)
    partial[:, :, 0:low] = dh[:, :, 0:low]
    partial[:, :, low:high] += dh[:, :, low:high]

    pair_base, quad_base, share_base, side_base = (next(base) for _ in range(4))
    others = [lax.rem(zh + k, Z) for k in range(1, Z)]
    for q in [*others, zh]:
        pair_out[q] = partial[q * 2 + 1 - core].astype(BF16)
        send(pair_out.at[q], pair_in.at[q], pair_base + q, pair_base + q, {"col": sibling})
    for q in others:
        receive(pair_in.at[q], pair_base + q, {"col": sibling})
        quad_out[q] = (partial[q * 2 + core] + pair_in[q].astype(F32)).astype(BF16)
        send(quad_out.at[q], quad_in.at[zh], quad_base + q, quad_base + zh, {"col": q * 2 + core})
    receive(pair_in.at[zh], pair_base + zh, {"col": sibling})
    total = partial[col] + pair_in[zh].astype(F32)
    for q in others:
        receive(quad_in.at[q], quad_base + q, {"col": q * 2 + core})
        total = total + quad_in[q].astype(F32)

    inv = lax.rsqrt(total[:, spare : spare + 1] / D + EPSILON)
    dh = total[:, 0:fh]
    gate = inv * total[:, fh : 2 * fh]
    up = inv * total[:, 2 * fh : 3 * fh]
    sigma = jax.nn.sigmoid(gate)
    act = gate * sigma
    d_gate = dh * up * sigma * (1.0 + gate * (1.0 - sigma))
    d_up = dh * act
    inner = inv * inv * jnp.sum(d_gate * gate + d_up * up, axis=1, keepdims=True)
    lane = lax.broadcasted_iota(jnp.int32, (total.shape[0], LANES), 1)
    act_all[col, :, last:fw] = jnp.where(lane == spare - last, inner, 0.0).astype(BF16)
    act_all[col, :, 0:fh] = (act * up).astype(BF16)
    act_all[col, :, fh : 2 * fh] = (inv * d_gate).astype(BF16)
    act_all[col, :, 2 * fh : 3 * fh] = (inv * d_up).astype(BF16)

    def pass_on(q):
        ours = act_all.at[q * 2 + core]
        send(ours, ours, side_base + q, side_base + q, {"col": sibling})

    for q in others:
        send(act_all.at[col], act_all.at[col], share_base + q, share_base + zh, {"col": q * 2 + core})
    pass_on(zh)
    for q in others:
        receive(act_all.at[q * 2 + core], share_base + q, {"col": q * 2 + core})
        pass_on(q)
    for q in [zh, *others]:
        receive(act_all.at[q * 2 + 1 - core], side_base + q, {"col": sibling})

    acts = act_all[...].reshape(tokens, fw)
    out_send[...] = dot(acts[:, 0:high], w_down[...]).astype(BF16).reshape(out_send.shape)
    o1 = exchange("depth", next(base), lambda p: out_send.at[p], lambda q: out_recv.at[q])
    act_rows[...] = dot(to_row, acts[:, low:fw]).astype(BF16)
    dn_send[:, :, 0:wide] = dot(act_rows[...], w_both[low:fw, :]).astype(BF16).reshape(R, Y * mine, wide)
    dn_send[:, :, wide : wide + LANES] = act_rows[:, last - low : fw - low].reshape(R, Y * mine, LANES)
    e1 = exchange("row", next(base), lambda p: dn_send.at[p], lambda q: dn_recv.at[q])
    out_recv[dep] = out_send[dep]
    dn_recv[row] = dn_send[row]

    flipped = jnp.transpose(acts)
    gd_out[...] = dot(flipped[0:fh], mixed_all[...]).astype(BF16)
    gg_out[...] = dot(flipped[fh : 2 * fh], normed[:, 0:wide]).astype(BF16)
    gu_out[...] = dot(flipped[2 * fh : 3 * fh], normed[:, 0:wide]).astype(BF16)
    stores = [
        pltpu.make_async_copy(gd_out, gd_hbm, local_sem.at[0]),
        pltpu.make_async_copy(gg_out, gg_hbm, local_sem.at[1]),
        pltpu.make_async_copy(gu_out, gu_hbm, local_sem.at[2]),
    ]
    for copy in stores:
        copy.start()

    def add(ref, n):
        total = ref[0].astype(F32)
        for q in range(1, n):
            total = total + ref[q].astype(F32)
        return total

    e1()
    total = add(dn_recv, R)
    for q in range(Y):
        dn_send2[q] = total[q * mine : (q + 1) * mine].astype(BF16)
    e2 = exchange("depth", next(base), lambda p: dn_send2.at[p], lambda q: dn_recv2.at[q])
    dn_recv2[dep] = dn_send2[dep]
    o1()
    total = add(out_recv, Y)
    for q in range(R):
        out_send2[q] = total[q * mine : (q + 1) * mine].astype(BF16)
    o2 = exchange("row", next(base), lambda p: out_send2.at[p], lambda q: out_recv2.at[q])
    out_recv2[row] = out_send2[row]

    e2()
    total = add(dn_recv2, Y)
    inner = total[:, wide + spare - last : wide + spare - last + 1]
    dstream_out[...] = (
        mixed_ref[...].astype(F32) + gain_ref[...] * total[:, 0:wide] - stream * (inner / D)
    ).astype(BF16)
    o2()
    new_out[...] = (stream + add(out_recv2, R)).astype(BF16)
    stores += [
        pltpu.make_async_copy(dstream_out, dstream_hbm, local_sem.at[3]),
        pltpu.make_async_copy(new_out, new_hbm, local_sem.at[4]),
    ]
    for copy in stores[3:]:
        copy.start()

    for copy in sent:
        copy.wait_send()
    for copy in stores:
        copy.wait()


def on_device(axes, stream, norm_gain, w_gate, w_up, w_down, d_mixed):
    R, C, Y = axes
    mine, wide = stream.shape
    fh = w_gate.shape[1]
    fw = (3 * fh // LANES + 1) * LANES
    low, high = fh // LANES * LANES, pl.cdiv(fh, LANES) * LANES
    width = wide + LANES
    tokens = R * Y * mine
    assert Y == C
    share = tokens // C
    Z = C // 2
    vmem = lambda *shape: pltpu.VMEM(shape, BF16)
    far = pl.BlockSpec(memory_space=pl.ANY)
    shape = lambda *a: jax.ShapeDtypeStruct(a, BF16)
    new, dstream, gg, gu, gd = pl.pallas_call(
        functools.partial(kernel, (R, C, Y, fh, wide * C)),
        out_shape=(
            shape(mine, wide),
            shape(mine, wide),
            shape(fh, wide),
            shape(fh, wide),
            shape(fh, wide),
        ),
        in_specs=[far] * 6,
        out_specs=[far] * 5,
        scratch_shapes=[
            vmem(mine, wide), vmem(mine, wide), pltpu.VMEM((1, wide), F32), vmem(high, wide), vmem(fw, wide),
            vmem(R, mine, width), vmem(Y, R * mine, width),
            vmem(Y, mine, wide), vmem(R, Y * mine, wide), vmem(tokens, wide),
            pltpu.VMEM((C, share, fw), F32),
            vmem(Z, share, fw), vmem(Z, share, fw), vmem(Z, share, fw), vmem(Z, share, fw),
            vmem(C, share, fw), vmem(tokens, fw - low),
            vmem(Y, R * mine, wide), vmem(Y, R * mine, wide), vmem(R, mine, wide), vmem(R, mine, wide),
            vmem(R, Y * mine, width), vmem(R, Y * mine, width), vmem(Y, mine, width), vmem(Y, mine, width),
            vmem(mine, wide), vmem(mine, wide), vmem(fh, wide), vmem(fh, wide), vmem(fh, wide),
            pltpu.SemaphoreType.DMA((6,)),
            pltpu.SemaphoreType.DMA((96,)),
            pltpu.SemaphoreType.DMA((96,)),
        ],
        compiler_params=pltpu.CompilerParams(
            collective_id=0, has_side_effects=True, vmem_limit_bytes=60 << 20
        ),
    )(stream, d_mixed, norm_gain.reshape(1, wide), w_gate.T, w_up.T, w_down)
    return new, dstream, gg.T, gu.T, gd


def solution(mesh):
    tokens, weights = P(("row", "depth"), "col"), P("col", ("row", "depth"))
    return jax.shard_map(
        functools.partial(on_device, tuple(mesh.shape[a] for a in ("row", "col", "depth"))),
        mesh=mesh,
        in_specs=(tokens, P("col"), weights, weights, tokens, tokens),
        out_specs=(tokens, tokens, weights, weights, tokens),
        check_vma=False,
    )
```

```python
import functools

import jax
import jax.numpy as jnp
from jax import lax
from jax.experimental import pallas as pl
from jax.experimental.pallas import tpu as pltpu
from jax.sharding import PartitionSpec as P

F32, BF16 = jnp.float32, jnp.bfloat16
LANES = 128
EPSILON = 1e-05


def dot(a, b, dims=((1,), (0,))):
    return lax.dot_general(a, b, (dims, ((), ())), preferred_element_type=F32)


def kernel(
    sizes,
    stream_hbm, mixed_hbm, gain_hbm, wg_hbm, wu_hbm, wd_hbm,
    new_hbm, dstream_hbm, gg_hbm, gu_hbm, gd_hbm,
    stream_ref, mixed_ref, gain_ref, w_down, w_both, wt_down, wt_both,
    norm_parts, norm_all, extra_parts, extra_rows, extra_all,
    partial, pair_in, quad_out, quad_in,
    act_all,
    out_send, out_recv, out_send2, out_recv2,
    dn_send, dn_recv, dn_send2, dn_recv2,
    new_out, dstream_out, gg_out, gu_out, gd_out,
    local_sem, send_sem, recv_sem,
):
    R, C, Y, fh, D = sizes
    mine, wide = stream_ref.shape
    head = norm_all.shape[3]
    fw = act_all.shape[4]
    low, high = fh // LANES * LANES, pl.cdiv(fh, LANES) * LANES
    spare = 3 * fh
    last = fw - LANES
    end = 2 * wide - head
    Z, X = C // 2, R // 2
    half = X * Y * mine
    row, col, dep = (lax.axis_index(a) for a in ("row", "col", "depth"))
    zh, core = lax.div(col, 2), lax.rem(col, 2)
    plane, x = lax.div(row, X), lax.rem(row, X)
    planes = (plane, 1 - plane)
    x_peers = [lax.rem(x + k, X) for k in range(1, X)]
    depths = [lax.rem(dep + k, Y) for k in range(1, Y)]
    others = [lax.rem(zh + k, Z) for k in range(1, Z)]
    across = (1 - plane) * X
    to_x = lambda q: {"row": plane * X + q}
    to_depth = lambda q: {"depth": q}
    to_plane = {"row": across + x}
    to_chip = lambda q: {"col": q * 2 + core}
    to_core = {"col": zh * 2 + 1 - core}
    peers = [to_plane, to_core]
    peers += [to_x(q) for q in x_peers] + [{"row": across + q} for q in x_peers]
    peers += [to_chip(q) for q in others] + [to_depth(q) for q in depths]
    peers += [{"row": across + x, "depth": q} for q in depths]
    barrier = pltpu.get_barrier_semaphore()
    for peer in peers:
        pl.semaphore_signal(barrier, 1, device_id=peer)

    loads = [
        pltpu.make_async_copy(a, b, local_sem.at[i])
        for i, (a, b) in enumerate([
            (stream_hbm, stream_ref),
            (gain_hbm, gain_ref),
            (mixed_hbm, mixed_ref),
            (wg_hbm, w_both.at[pl.ds(fh, fh)]),
            (wu_hbm, w_both.at[pl.ds(2 * fh, fh)]),
            (wd_hbm, w_down.at[pl.ds(0, fh)]),
        ])
    ]
    for copy in loads:
        copy.start()

    sent, slots, waited = [], iter(range(160)), []

    def take(n):
        return [next(slots) for _ in range(n)][0]

    def send(src, dst, slot, to):
        copy = pltpu.make_async_remote_copy(
            src_ref=src, dst_ref=dst,
            send_sem=send_sem.at[len(waited) + len(sent)], recv_sem=recv_sem.at[slot], device_id=to,
        )
        copy.start()
        sent.append(copy)

    def receive(dst, slot, to):
        pltpu.make_async_remote_copy(
            src_ref=dst, dst_ref=dst,
            send_sem=send_sem.at[0], recv_sem=recv_sem.at[slot], device_id=to,
        ).wait_recv()

    def drain():
        for copy in sent:
            copy.wait_send()
        waited.extend(sent)
        sent.clear()

    def exchange(others, me, to, source, target, n):
        slot = take(n)
        for q in others:
            send(source(q), target(me), slot + me, to(q))

        def finish():
            for q in others:
                receive(target(q), slot + q, to(q))

        return finish

    for copy in loads[:3]:
        copy.wait()
    stream = stream_ref[...].astype(F32)
    scaled = (stream * gain_ref[...]).astype(BF16)
    squares = jnp.sum(stream * stream, axis=1, keepdims=True)
    lane = lax.broadcasted_iota(jnp.int32, (mine, LANES), 1)
    norm_parts[x] = scaled[:, 0:head]
    extra_parts[dep, :, 0:wide] = mixed_ref[...]
    extra_parts[dep, :, wide:end] = scaled[:, head:wide]
    extra_parts[dep, :, end : end + LANES] = jnp.where(
        lane == spare - last, squares, 0.0
    ).astype(BF16)

    pl.semaphore_wait(barrier, len(peers))
    n1 = exchange(x_peers, x, to_x, lambda q: norm_parts.at[x], lambda q: norm_parts.at[q], X)
    d1 = exchange(depths, dep, to_depth, lambda q: extra_parts.at[dep], lambda q: extra_parts.at[q], Y)
    n1()
    norm_all[plane, dep] = norm_parts[...].astype(F32).reshape(norm_all.shape[2:]).astype(BF16)
    over = take(2)
    ours = norm_all.at[plane, dep]
    send(ours, ours, over, to_plane)

    def spread_norm(p):
        return exchange(depths, dep, to_depth, lambda q: norm_all.at[p, dep], lambda q: norm_all.at[p, q], Y)

    def spread_extra(p):
        return exchange(x_peers, x, to_x, lambda q: extra_rows.at[p, x], lambda q: extra_rows.at[p, q], X)

    n2 = [spread_norm(plane)]
    d1()
    extra_rows[plane, x] = extra_parts[...].astype(F32).reshape(extra_rows.shape[2:]).astype(BF16)
    ours = extra_rows.at[plane, x]
    send(ours, ours, over + 1, to_plane)
    d2 = [spread_extra(plane)]

    for copy in loads[3:]:
        copy.wait()
    w_down[fh:high, :] = jnp.zeros((high - fh, wide), BF16)
    w_both[low:fh, :] = jnp.zeros((fh - low, wide), BF16)
    w_both[spare:fw, :] = jnp.zeros((fw - spare, wide), BF16)
    wt_both[...] = jnp.transpose(w_both[low:fw, :])
    wt_down[...] = jnp.transpose(w_down[...])
    t = lax.broadcasted_iota(jnp.int32, (half, half), 0)
    u = lax.broadcasted_iota(jnp.int32, (half, half), 1)
    there = ((t // mine) % X) * (Y * mine) + (t // (X * mine)) * mine + t % mine
    by_depth = (u == there).astype(F32).astype(BF16)
    there = ((t // mine) % Y) * (X * mine) + (t // (Y * mine)) * mine + t % mine
    by_x = (u == there).astype(F32).astype(BF16)

    drain()
    receive(norm_all.at[1 - plane, dep], over, to_plane)
    n2.append(spread_norm(1 - plane))
    receive(extra_rows.at[1 - plane, x], over + 1, to_plane)
    d2.append(spread_extra(1 - plane))

    quad = []
    for h, p in enumerate(planes):
        n2[h]()
        d2[h]()
        extra = dot(by_depth, extra_rows[p].reshape(half, end + LANES)).astype(BF16)
        extra_all[p] = extra
        both = dot(norm_all[p].reshape(half, head), wt_both[0:head, :])
        both += dot(extra[:, wide:end], wt_both[head:wide, :])
        both = both.reshape(2, Z, X * mine, fw - low)
        partial[p, :, :, :, low:fw] = both
        partial[p, :, :, :, last:fw] += extra[:, end : end + LANES].astype(F32).reshape(2, Z, X * mine, LANES)
        dh = dot(extra[:, 0:wide], wt_down[...]).reshape(2, Z, X * mine, high)
        partial[p, :, :, :, 0:low] = dh[:, :, :, 0:low]
        partial[p, :, :, :, low:high] += dh[:, :, :, low:high]
        pair = take(1)
        send(partial.at[p, 1 - core], pair_in.at[p], pair, to_core)
        receive(pair_in.at[p], pair, to_core)
        for q in others:
            quad_out[p, q] = (partial[p, core, q] + pair_in[p, q]).astype(BF16)
        quad.append(exchange(others, zh, to_chip, lambda q: quad_out.at[p, q], lambda q, p=p: quad_in.at[p, q], Z))

    share = []
    for h, p in enumerate(planes):
        quad[h]()
        total = partial[p, core, zh] + pair_in[p, zh]
        for q in others:
            total = total + quad_in[p, q].astype(F32)
        inv = lax.rsqrt(total[:, spare : spare + 1] / D + EPSILON)
        dh = total[:, 0:fh]
        gate = inv * total[:, fh : 2 * fh]
        up = inv * total[:, 2 * fh : 3 * fh]
        sigma = jax.nn.sigmoid(gate)
        act = gate * sigma
        d_gate = dh * up * sigma * (1.0 + gate * (1.0 - sigma))
        d_up = dh * act
        inner = inv * inv * jnp.sum(d_gate * gate + d_up * up, axis=1, keepdims=True)
        lane = lax.broadcasted_iota(jnp.int32, (total.shape[0], LANES), 1)
        act_all[p, core, zh, :, last:fw] = jnp.where(lane == spare - last, inner, 0.0).astype(BF16)
        act_all[p, core, zh, :, 0:fh] = (act * up).astype(BF16)
        act_all[p, core, zh, :, fh : 2 * fh] = (inv * d_gate).astype(BF16)
        act_all[p, core, zh, :, 2 * fh : 3 * fh] = (inv * d_up).astype(BF16)
        share.append(exchange(others, zh, to_chip, lambda q: act_all.at[p, core, zh], lambda q, p=p: act_all.at[p, core, q], Z))

    e1, o1 = [], []
    for h, p in enumerate(planes):
        side = take(1)
        share[h]()
        send(act_all.at[p, core], act_all.at[p, core], side, to_core)
        receive(act_all.at[p, 1 - core], side, to_core)
        acts = act_all[p].reshape(half, fw)
        out_send[p] = dot(acts[:, 0:high], w_down[:, 0:head]).astype(BF16).reshape(Y, X * mine, head)
        o1.append(exchange(depths, dep, to_depth, lambda q: out_send.at[p, q], lambda q, p=p: out_recv.at[p, q], Y))
        acts = dot(by_x, acts).astype(BF16)
        dn_send[p, :, :, 0:wide] = dot(acts[:, low:fw], w_both[low:fw, :]).astype(BF16).reshape(X, Y * mine, wide)
        dn_send[p, :, :, wide:end] = dot(acts[:, 0:high], w_down[:, head:wide]).astype(BF16).reshape(X, Y * mine, wide - head)
        dn_send[p, :, :, end : end + LANES] = acts[:, last:fw].reshape(X, Y * mine, LANES)
        e1.append(exchange(x_peers, x, to_x, lambda q: dn_send.at[p, q], lambda q, p=p: dn_recv.at[p, q], X))
        out_recv[p, dep] = out_send[p, dep]
        dn_recv[p, x] = dn_send[p, x]

    flipped = jnp.transpose(act_all[...].reshape(2 * half, fw))
    extra = extra_all[...].reshape(2 * half, end + LANES)
    normed = norm_all[...].reshape(2 * half, head)
    gd_out[...] = dot(flipped[0:fh], extra[:, 0:wide]).astype(BF16)
    stores = [pltpu.make_async_copy(gd_out, gd_hbm, local_sem.at[0])]
    stores[0].start()
    for i, (out, hbm) in enumerate(((gg_out, gg_hbm), (gu_out, gu_hbm)), 1):
        out[:, 0:head] = dot(flipped[i * fh : (i + 1) * fh], normed).astype(BF16)
        out[:, head:wide] = dot(flipped[i * fh : (i + 1) * fh], extra[:, wide:end]).astype(BF16)
        stores.append(pltpu.make_async_copy(out, hbm, local_sem.at[i]))
        stores[i].start()

    def add(ref, n):
        total = ref[0].astype(F32)
        for q in range(1, n):
            total = total + ref[q].astype(F32)
        return total

    def split(total, ref, n):
        for q in range(n):
            ref[q] = total[q * mine : (q + 1) * mine].astype(BF16)

    e2, o2 = take(2 * Y), take(2 * X)
    for h, p in enumerate(planes):
        e1[h]()
        split(add(dn_recv.at[p], X), dn_send2.at[p], Y)
        for q in depths if h == 0 else [dep, *depths]:
            to = {"depth": q} if h == 0 else {"row": across + x, "depth": q}
            send(dn_send2.at[p, q], dn_recv2.at[plane, dep], e2 + plane * Y + dep, to)
        o1[h]()
        split(add(out_recv.at[p], Y), out_send2.at[p], X)
        for q in x_peers if h == 0 else [x, *x_peers]:
            send(out_send2.at[p, q], out_recv2.at[plane, x], o2 + plane * X + x, {"row": p * X + q})
    out_recv2[plane, x] = out_send2[plane, x]
    dn_recv2[plane, dep] = dn_send2[plane, dep]

    for h, p in enumerate(planes):
        for q in x_peers if h == 0 else [x, *x_peers]:
            receive(out_recv2.at[p, q], o2 + p * X + q, {"row": p * X + q})
    total = add(out_recv2.at[0], X) + add(out_recv2.at[1], X)
    new_out[:, 0:head] = (stream[:, 0:head] + total).astype(BF16)
    for h, p in enumerate(planes):
        for q in depths if h == 0 else [dep, *depths]:
            to = {"depth": q} if h == 0 else {"row": across + x, "depth": q}
            receive(dn_recv2.at[p, q], e2 + p * Y + q, to)
    total = add(dn_recv2.at[0], Y) + add(dn_recv2.at[1], Y)
    inner = total[:, end + spare - last : end + spare - last + 1]
    dstream_out[...] = (
        mixed_ref[...].astype(F32) + gain_ref[...] * total[:, 0:wide] - stream * (inner / D)
    ).astype(BF16)
    new_out[:, head:wide] = (stream[:, head:wide] + total[:, wide:end]).astype(BF16)
    stores += [
        pltpu.make_async_copy(dstream_out, dstream_hbm, local_sem.at[3]),
        pltpu.make_async_copy(new_out, new_hbm, local_sem.at[4]),
    ]
    for copy in stores[3:]:
        copy.start()

    drain()
    for copy in stores:
        copy.wait()


def hand_over(*refs):
    n = len(refs) // 3
    given, out, held, (sem,) = refs[:n], refs[n : 2 * n], refs[2 * n : 3 * n], refs[3 * n :]
    loads = [pltpu.make_async_copy(given[i], held[i], sem.at[i]) for i in range(n)]
    stores = [pltpu.make_async_copy(held[i], out[i], sem.at[n + i]) for i in range(n)]
    for copy in loads:
        copy.start()
    for load, store in zip(loads, stores):
        load.wait()
        store.start()
    for copy in stores:
        copy.wait()


def on_device(axes, stream, norm_gain, w_gate, w_up, w_down, d_mixed):
    R, C, Y = axes
    mine, wide = stream.shape
    fh = w_gate.shape[1]
    fw = (3 * fh // LANES + 1) * LANES
    low, high = fh // LANES * LANES, pl.cdiv(fh, LANES) * LANES
    head = wide // LANES * 3 // 4 * LANES
    both = 2 * wide - head + LANES
    Z, X = C // 2, R // 2
    assert Y == C
    half = X * Y * mine
    vmem = lambda *shape: pltpu.VMEM(shape, BF16)
    f32 = lambda *shape: pltpu.VMEM(shape, F32)
    far = pl.BlockSpec(memory_space=pltpu.HBM)
    shape = lambda *a: jax.ShapeDtypeStruct(a, BF16)
    shapes = (shape(mine, wide),) * 2 + (shape(fh, wide),) * 3
    outs = pl.pallas_call(
        functools.partial(kernel, (R, C, Y, fh, wide * C)),
        out_shape=shapes,
        in_specs=[far] * 6,
        out_specs=[far] * 5,
        scratch_shapes=[
            vmem(mine, wide), vmem(mine, wide), f32(1, wide),
            vmem(high, wide), vmem(fw, wide), vmem(wide, high), vmem(wide, fw - low),
            vmem(X, mine, head), vmem(2, Y, X * mine, head),
            vmem(Y, mine, both), vmem(2, X, Y * mine, both), vmem(2, half, both),
            f32(2, 2, Z, X * mine, fw), f32(2, Z, X * mine, fw),
            vmem(2, Z, X * mine, fw), vmem(2, Z, X * mine, fw),
            vmem(2, 2, Z, X * mine, fw),
            vmem(2, Y, X * mine, head), vmem(2, Y, X * mine, head), vmem(2, X, mine, head), vmem(2, X, mine, head),
            vmem(2, X, Y * mine, both), vmem(2, X, Y * mine, both), vmem(2, Y, mine, both), vmem(2, Y, mine, both),
            vmem(mine, wide), vmem(mine, wide), vmem(fh, wide), vmem(fh, wide), vmem(fh, wide),
            pltpu.SemaphoreType.DMA((6,)),
            pltpu.SemaphoreType.DMA((160,)),
            pltpu.SemaphoreType.DMA((160,)),
        ],
        compiler_params=pltpu.CompilerParams(
            collective_id=0, has_side_effects=True, vmem_limit_bytes=60 << 20
        ),
    )(stream, d_mixed, norm_gain.reshape(1, wide), w_gate.T, w_up.T, w_down)
    new, dstream, gg, gu, gd = pl.pallas_call(
        hand_over,
        out_shape=shapes,
        in_specs=[far] * 5,
        out_specs=[far] * 5,
        scratch_shapes=[*(vmem(*a.shape) for a in shapes), pltpu.SemaphoreType.DMA((10,))],
        compiler_params=pltpu.CompilerParams(vmem_limit_bytes=60 << 20),
    )(*outs)
    return new, dstream, gg.T, gu.T, gd


def solution(mesh):
    tokens, weights = P(("row", "depth"), "col"), P("col", ("row", "depth"))
    return jax.shard_map(
        functools.partial(on_device, tuple(mesh.shape[a] for a in ("row", "col", "depth"))),
        mesh=mesh,
        in_specs=(tokens, P("col"), weights, weights, tokens, tokens),
        out_specs=(tokens, tokens, weights, weights, tokens),
        check_vma=False,
    )
```

```python
import functools

import jax
import jax.numpy as jnp
from jax import lax
from jax.experimental import pallas as pl
from jax.experimental.pallas import tpu as pltpu
from jax.sharding import PartitionSpec as P

F32, BF16 = jnp.float32, jnp.bfloat16
LANES = 128
EPSILON = 1e-05


def dot(a, b, dims=((1,), (0,))):
    return lax.dot_general(a, b, (dims, ((), ())), preferred_element_type=F32)


def kernel(
    sizes,
    stream_hbm, mixed_hbm, gain_hbm, wg_hbm, wu_hbm, wd_hbm,
    new_out, dstream_out, gg_out, gu_out, gd_out,
    stream_ref, mixed_ref, gain_ref, w_down, w_both, wt_down, wt_both,
    norm_parts, norm_all, extra_parts, extra_rows, extra_all,
    partial, pair_in, quad_out, quad_in,
    act_all,
    out_send, out_recv, out_send2, out_recv2,
    dn_send, dn_recv, dn_send2, dn_recv2,
    local_sem, send_sem, recv_sem,
):
    R, C, Y, fh, D = sizes
    mine, wide = stream_ref.shape
    head = norm_all.shape[3]
    fw = act_all.shape[4]
    low, high = fh // LANES * LANES, pl.cdiv(fh, LANES) * LANES
    spare = 3 * fh
    last = fw - LANES
    end = 2 * wide - head
    Z, X = C // 2, R // 2
    half = X * Y * mine
    row, col, dep = (lax.axis_index(a) for a in ("row", "col", "depth"))
    zh, core = lax.div(col, 2), lax.rem(col, 2)
    plane, x = lax.div(row, X), lax.rem(row, X)
    planes = (plane, 1 - plane)
    loads = [
        pltpu.make_async_copy(a, b, local_sem.at[i])
        for i, (a, b) in enumerate([
            (stream_hbm, stream_ref),
            (gain_hbm, gain_ref),
            (mixed_hbm, mixed_ref),
            (wg_hbm, w_both.at[pl.ds(fh, fh)]),
            (wu_hbm, w_both.at[pl.ds(2 * fh, fh)]),
            (wd_hbm, w_down.at[pl.ds(0, fh)]),
        ])
    ]
    for copy in loads[:3]:
        copy.start()

    far = lambda n: sorted(range(1, n), key=lambda k: abs(k - n // 2))
    x_peers = [lax.rem(x + k, X) for k in far(X)]
    depths = [lax.rem(dep + k, Y) for k in far(Y)]
    others = [lax.rem(zh + k, Z) for k in far(Z)]
    across = (1 - plane) * X
    to_x = lambda q: {"row": plane * X + q}
    to_depth = lambda q: {"depth": q}
    to_plane = {"row": across + x}
    to_chip = lambda q: {"col": q * 2 + core}
    to_core = {"col": zh * 2 + 1 - core}
    peers = [to_plane, to_core]
    peers += [to_x(q) for q in x_peers] + [{"row": across + q} for q in x_peers]
    peers += [to_chip(q) for q in others] + [to_depth(q) for q in depths]
    peers += [{"row": across + x, "depth": q} for q in depths]
    barrier = pltpu.get_barrier_semaphore()
    for peer in peers:
        pl.semaphore_signal(barrier, 1, device_id=peer)
    for copy in loads[3:]:
        copy.start()

    sent, slots, waited = [], iter(range(160)), []

    def take(n):
        return [next(slots) for _ in range(n)][0]

    def send(src, dst, slot, to):
        copy = pltpu.make_async_remote_copy(
            src_ref=src, dst_ref=dst,
            send_sem=send_sem.at[len(waited) + len(sent)], recv_sem=recv_sem.at[slot], device_id=to,
        )
        copy.start()
        sent.append(copy)

    def receive(dst, slot, to):
        pltpu.make_async_remote_copy(
            src_ref=dst, dst_ref=dst,
            send_sem=send_sem.at[0], recv_sem=recv_sem.at[slot], device_id=to,
        ).wait_recv()

    def drain(n=None):
        for copy in sent[:n]:
            copy.wait_send()
        waited.extend(sent[:n])
        del sent[:n]

    def exchange(others, me, to, source, target, n):
        slot = take(n)
        for q in others:
            send(source(q), target(me), slot + me, to(q))

        def finish():
            for q in others:
                receive(target(q), slot + q, to(q))

        return finish

    for copy in loads[:3]:
        copy.wait()
    stream = stream_ref[...].astype(F32)
    scaled = (stream * gain_ref[...]).astype(BF16)
    squares = jnp.sum(stream * stream, axis=1, keepdims=True)
    lane = lax.broadcasted_iota(jnp.int32, (mine, LANES), 1)
    norm_parts[x] = scaled[:, 0:head]
    extra_parts[dep, :, 0:wide] = mixed_ref[...]
    extra_parts[dep, :, wide:end] = scaled[:, head:wide]
    extra_parts[dep, :, end : end + LANES] = jnp.where(
        lane == spare - last, squares, 0.0
    ).astype(BF16)

    pl.semaphore_wait(barrier, len(peers))
    n1 = exchange(x_peers, x, to_x, lambda q: norm_parts.at[x], lambda q: norm_parts.at[q], X)
    d1 = exchange(depths, dep, to_depth, lambda q: extra_parts.at[dep], lambda q: extra_parts.at[q], Y)
    n1()
    norm_all[plane, dep] = norm_parts[...].astype(F32).reshape(norm_all.shape[2:]).astype(BF16)
    over = take(2)
    ours = norm_all.at[plane, dep]
    send(ours, ours, over, to_plane)

    def spread_norm(p):
        return exchange(depths, dep, to_depth, lambda q: norm_all.at[p, dep], lambda q: norm_all.at[p, q], Y)

    def spread_extra(p):
        return exchange(x_peers, x, to_x, lambda q: extra_rows.at[p, x], lambda q: extra_rows.at[p, q], X)

    n2 = [spread_norm(plane)]
    d1()
    extra_rows[plane, x] = extra_parts[...].astype(F32).reshape(extra_rows.shape[2:]).astype(BF16)
    ours = extra_rows.at[plane, x]
    send(ours, ours, over + 1, to_plane)
    d2 = [spread_extra(plane)]

    for copy in loads[3:]:
        copy.wait()
    w_down[fh:high, :] = jnp.zeros((high - fh, wide), BF16)
    w_both[low:fh, :] = jnp.zeros((fh - low, wide), BF16)
    w_both[spare:fw, :] = jnp.zeros((fw - spare, wide), BF16)
    wt_both[...] = jnp.transpose(w_both[low:fw, :])
    wt_down[...] = jnp.transpose(w_down[...])
    t = lax.broadcasted_iota(jnp.int32, (half, half), 0)
    u = lax.broadcasted_iota(jnp.int32, (half, half), 1)
    there = ((t // mine) % X) * (Y * mine) + (t // (X * mine)) * mine + t % mine
    by_depth = (u == there).astype(F32).astype(BF16)
    there = ((t // mine) % Y) * (X * mine) + (t // (Y * mine)) * mine + t % mine
    by_x = (u == there).astype(F32).astype(BF16)

    drain(-3)
    receive(norm_all.at[1 - plane, dep], over, to_plane)
    n2.append(spread_norm(1 - plane))
    receive(extra_rows.at[1 - plane, x], over + 1, to_plane)
    d2.append(spread_extra(1 - plane))

    quad = []
    for h, p in enumerate(planes):
        n2[h]()
        d2[h]()
        extra = dot(by_depth, extra_rows[p].reshape(half, end + LANES)).astype(BF16)
        extra_all[p] = extra
        both = dot(norm_all[p].reshape(half, head), wt_both[0:head, :])
        both += dot(extra[:, wide:end], wt_both[head:wide, :])
        both = both.reshape(2, Z, X * mine, fw - low)
        partial[p, :, :, :, low:fw] = both
        partial[p, :, :, :, last:fw] += extra[:, end : end + LANES].astype(F32).reshape(2, Z, X * mine, LANES)
        dh = dot(extra[:, 0:wide], wt_down[...]).reshape(2, Z, X * mine, high)
        partial[p, :, :, :, 0:low] = dh[:, :, :, 0:low]
        partial[p, :, :, :, low:high] += dh[:, :, :, low:high]
        pair = take(1)
        send(partial.at[p, 1 - core], pair_in.at[p], pair, to_core)
        receive(pair_in.at[p], pair, to_core)
        for q in others:
            quad_out[p, q] = (partial[p, core, q] + pair_in[p, q]).astype(BF16)
        quad.append(exchange(others, zh, to_chip, lambda q: quad_out.at[p, q], lambda q, p=p: quad_in.at[p, q], Z))

    share = []
    for h, p in enumerate(planes):
        quad[h]()
        total = partial[p, core, zh] + pair_in[p, zh]
        for q in others:
            total = total + quad_in[p, q].astype(F32)
        inv = lax.rsqrt(total[:, spare : spare + 1] / D + EPSILON)
        dh = total[:, 0:fh]
        gate = inv * total[:, fh : 2 * fh]
        up = inv * total[:, 2 * fh : 3 * fh]
        sigma = jax.nn.sigmoid(gate)
        act = gate * sigma
        d_gate = dh * up * sigma * (1.0 + gate * (1.0 - sigma))
        d_up = dh * act
        inner = inv * inv * jnp.sum(d_gate * gate + d_up * up, axis=1, keepdims=True)
        lane = lax.broadcasted_iota(jnp.int32, (total.shape[0], LANES), 1)
        act_all[p, core, zh, :, last:fw] = jnp.where(lane == spare - last, inner, 0.0).astype(BF16)
        act_all[p, core, zh, :, 0:fh] = (act * up).astype(BF16)
        act_all[p, core, zh, :, fh : 2 * fh] = (inv * d_gate).astype(BF16)
        act_all[p, core, zh, :, 2 * fh : 3 * fh] = (inv * d_up).astype(BF16)
        share.append(exchange(others, zh, to_chip, lambda q: act_all.at[p, core, zh], lambda q, p=p: act_all.at[p, core, q], Z))

    e1, o1 = [], []
    for h, p in enumerate(planes):
        side = take(1)
        share[h]()
        send(act_all.at[p, core], act_all.at[p, core], side, to_core)
        receive(act_all.at[p, 1 - core], side, to_core)
        acts = act_all[p].reshape(half, fw)
        out_send[p] = dot(acts[:, 0:high], w_down[:, 0:head]).astype(BF16).reshape(Y, X * mine, head)
        o1.append(exchange(depths, dep, to_depth, lambda q: out_send.at[p, q], lambda q, p=p: out_recv.at[p, q], Y))
        acts = dot(by_x, acts).astype(BF16)
        dn_send[p, :, :, 0:wide] = dot(acts[:, low:fw], w_both[low:fw, :]).astype(BF16).reshape(X, Y * mine, wide)
        dn_send[p, :, :, wide:end] = dot(acts[:, 0:high], w_down[:, head:wide]).astype(BF16).reshape(X, Y * mine, wide - head)
        dn_send[p, :, :, end : end + LANES] = acts[:, last:fw].reshape(X, Y * mine, LANES)
        e1.append(exchange(x_peers, x, to_x, lambda q: dn_send.at[p, q], lambda q, p=p: dn_recv.at[p, q], X))
        out_recv[p, dep] = out_send[p, dep]
        dn_recv[p, x] = dn_send[p, x]

    drain(-(len(depths) + len(x_peers)))

    flipped = jnp.transpose(act_all[...].reshape(2 * half, fw))
    extra = extra_all[...].reshape(2 * half, end + LANES)
    normed = norm_all[...].reshape(2 * half, head)
    gd_out[...] = dot(flipped[0:fh], extra[:, 0:wide]).astype(BF16)
    for i, out in ((1, gg_out), (2, gu_out)):
        out[:, 0:head] = dot(flipped[i * fh : (i + 1) * fh], normed).astype(BF16)
        out[:, head:wide] = dot(flipped[i * fh : (i + 1) * fh], extra[:, wide:end]).astype(BF16)

    def add(ref, n):
        total = ref[0].astype(F32)
        for q in range(1, n):
            total = total + ref[q].astype(F32)
        return total

    def split(total, ref, n):
        for q in range(n):
            ref[q] = total[q * mine : (q + 1) * mine].astype(BF16)

    e2, o2 = take(2 * Y), take(2 * X)
    for h, p in enumerate(planes):
        e1[h]()
        split(add(dn_recv.at[p], X), dn_send2.at[p], Y)
        for q in depths if h == 0 else [dep, *depths]:
            to = {"depth": q} if h == 0 else {"row": across + x, "depth": q}
            send(dn_send2.at[p, q], dn_recv2.at[plane, dep], e2 + plane * Y + dep, to)
        o1[h]()
        split(add(out_recv.at[p], Y), out_send2.at[p], X)
        for q in x_peers if h == 0 else [x, *x_peers]:
            send(out_send2.at[p, q], out_recv2.at[plane, x], o2 + plane * X + x, {"row": p * X + q})
    out_recv2[plane, x] = out_send2[plane, x]
    dn_recv2[plane, dep] = dn_send2[plane, dep]

    for h, p in enumerate(planes):
        for q in x_peers if h == 0 else [x, *x_peers]:
            receive(out_recv2.at[p, q], o2 + p * X + q, {"row": p * X + q})
    total = add(out_recv2.at[0], X) + add(out_recv2.at[1], X)
    new_out[:, 0:head] = (stream[:, 0:head] + total).astype(BF16)
    for h, p in enumerate(planes):
        for q in depths if h == 0 else [dep, *depths]:
            to = {"depth": q} if h == 0 else {"row": across + x, "depth": q}
            receive(dn_recv2.at[p, q], e2 + p * Y + q, to)
    total = add(dn_recv2.at[0], Y) + add(dn_recv2.at[1], Y)
    inner = total[:, end + spare - last : end + spare - last + 1]
    dstream_out[...] = (
        mixed_ref[...].astype(F32) + gain_ref[...] * total[:, 0:wide] - stream * (inner / D)
    ).astype(BF16)
    new_out[:, head:wide] = (stream[:, head:wide] + total[:, wide:end]).astype(BF16)

    drain()


def hand_over(*refs):
    n = len(refs) // 2
    copies = [pltpu.make_async_copy(refs[i], refs[n + i], refs[2 * n].at[i]) for i in range(n)]
    for copy in copies:
        copy.start()
    for copy in copies:
        copy.wait()


def on_device(axes, stream, norm_gain, w_gate, w_up, w_down, d_mixed):
    R, C, Y = axes
    mine, wide = stream.shape
    fh = w_gate.shape[1]
    fw = (3 * fh // LANES + 1) * LANES
    low, high = fh // LANES * LANES, pl.cdiv(fh, LANES) * LANES
    head = wide // LANES * 3 // 4 * LANES
    both = 2 * wide - head + LANES
    Z, X = C // 2, R // 2
    assert Y == C
    half = X * Y * mine
    vmem = lambda *shape: pltpu.VMEM(shape, BF16)
    f32 = lambda *shape: pltpu.VMEM(shape, F32)
    near = pl.BlockSpec(memory_space=pltpu.VMEM)
    far = pl.BlockSpec(memory_space=pltpu.HBM)
    shape = lambda *a: jax.ShapeDtypeStruct(a, BF16)
    shapes = (shape(mine, wide),) * 2 + (shape(fh, wide),) * 3
    outs = pl.pallas_call(
        functools.partial(kernel, (R, C, Y, fh, wide * C)),
        out_shape=tuple(pltpu.VMEM(a.shape, BF16) for a in shapes),
        in_specs=[far] * 6,
        out_specs=[near] * 5,
        scratch_shapes=[
            vmem(mine, wide), vmem(mine, wide), f32(1, wide),
            vmem(high, wide), vmem(fw, wide), vmem(wide, high), vmem(wide, fw - low),
            vmem(X, mine, head), vmem(2, Y, X * mine, head),
            vmem(Y, mine, both), vmem(2, X, Y * mine, both), vmem(2, half, both),
            f32(2, 2, Z, X * mine, fw), f32(2, Z, X * mine, fw),
            vmem(2, Z, X * mine, fw), vmem(2, Z, X * mine, fw),
            vmem(2, 2, Z, X * mine, fw),
            vmem(2, Y, X * mine, head), vmem(2, Y, X * mine, head), vmem(2, X, mine, head), vmem(2, X, mine, head),
            vmem(2, X, Y * mine, both), vmem(2, X, Y * mine, both), vmem(2, Y, mine, both), vmem(2, Y, mine, both),
            pltpu.SemaphoreType.DMA((6,)),
            pltpu.SemaphoreType.DMA((160,)),
            pltpu.SemaphoreType.DMA((160,)),
        ],
        compiler_params=pltpu.CompilerParams(
            collective_id=0, has_side_effects=True, vmem_limit_bytes=61 << 20
        ),
    )(stream, d_mixed, norm_gain.reshape(1, wide), w_gate.T, w_up.T, w_down)
    new, dstream, gg, gu, gd = pl.pallas_call(
        hand_over,
        out_shape=shapes,
        in_specs=[near] * 5,
        out_specs=[far] * 5,
        scratch_shapes=[pltpu.SemaphoreType.DMA((5,))],
        compiler_params=pltpu.CompilerParams(vmem_limit_bytes=1 << 20),
    )(*outs)
    return new, dstream, gg.T, gu.T, gd


def solution(mesh):
    tokens, weights = P(("row", "depth"), "col"), P("col", ("row", "depth"))
    return jax.shard_map(
        functools.partial(on_device, tuple(mesh.shape[a] for a in ("row", "col", "depth"))),
        mesh=mesh,
        in_specs=(tokens, P("col"), weights, weights, tokens, tokens),
        out_specs=(tokens, tokens, weights, weights, tokens),
        check_vma=False,
    )
```

```python
import functools

import jax
import jax.numpy as jnp
from jax import lax
from jax.experimental import pallas as pl
from jax.experimental.pallas import tpu as pltpu
from jax.sharding import PartitionSpec as P

F32, BF16 = jnp.float32, jnp.bfloat16
LANES = 128
EPSILON = 1e-05


def dot(a, b, dims=((1,), (0,))):
    return lax.dot_general(a, b, (dims, ((), ())), preferred_element_type=F32)


def kernel(
    sizes,
    stream_hbm, mixed_hbm, gain_hbm, wg_hbm, wu_hbm, wd_hbm,
    new_out, dstream_out, gg_out, gu_out, gd_out,
    stream_ref, mixed_ref, gain_ref, w_down, w_both, wt_down, wt_both,
    norm_parts, norm_all, extra_parts, extra_rows, extra_all,
    partial, pair_in, quad_out, quad_in,
    act_all,
    out_send, out_recv, out_send2, out_recv2,
    dn_send, dn_recv, dn_send2, dn_recv2,
    local_sem, send_sem, recv_sem,
):
    R, C, Y, fh, D = sizes
    mine, wide = stream_ref.shape
    head = norm_all.shape[3]
    fw = act_all.shape[4]
    low, high = fh // LANES * LANES, pl.cdiv(fh, LANES) * LANES
    spare = 3 * fh
    last = fw - LANES
    end = 2 * wide - head
    Z, X = C // 2, R // 2
    half = X * Y * mine
    row, col, dep = (lax.axis_index(a) for a in ("row", "col", "depth"))
    zh, core = lax.div(col, 2), lax.rem(col, 2)
    plane, x = lax.div(row, X), lax.rem(row, X)
    planes = (plane, 1 - plane)
    loads = [
        pltpu.make_async_copy(a, b, local_sem.at[i])
        for i, (a, b) in enumerate([
            (stream_hbm, stream_ref),
            (gain_hbm, gain_ref),
            (mixed_hbm, mixed_ref),
            (wg_hbm, w_both.at[pl.ds(fh, fh)]),
            (wu_hbm, w_both.at[pl.ds(2 * fh, fh)]),
            (wd_hbm, w_down.at[pl.ds(0, fh)]),
        ])
    ]
    for copy in loads[:3]:
        copy.start()

    far = lambda n: sorted(range(1, n), key=lambda k: abs(k - n // 2))
    x_peers = [lax.rem(x + k, X) for k in far(X)]
    depths = [lax.rem(dep + k, Y) for k in far(Y)]
    others = [lax.rem(zh + k, Z) for k in far(Z)]
    across = (1 - plane) * X
    to_x = lambda q: {"row": plane * X + q}
    to_depth = lambda q: {"depth": q}
    to_plane = {"row": across + x}
    to_chip = lambda q: {"col": q * 2 + core}
    to_core = {"col": zh * 2 + 1 - core}
    peers = [to_plane, to_core]
    peers += [to_x(q) for q in x_peers] + [{"row": across + q} for q in x_peers]
    peers += [to_chip(q) for q in others] + [to_depth(q) for q in depths]
    peers += [{"row": across + x, "depth": q} for q in depths]
    barrier = pltpu.get_barrier_semaphore()
    for peer in reversed(peers):
        pl.semaphore_signal(barrier, 1, device_id=peer)
    for copy in loads[3:]:
        copy.start()

    sent, slots, waited = [], iter(range(160)), []

    def take(n):
        return [next(slots) for _ in range(n)][0]

    def send(src, dst, slot, to):
        copy = pltpu.make_async_remote_copy(
            src_ref=src, dst_ref=dst,
            send_sem=send_sem.at[len(waited) + len(sent)], recv_sem=recv_sem.at[slot], device_id=to,
        )
        copy.start()
        sent.append(copy)

    def receive(dst, slot, to):
        pltpu.make_async_remote_copy(
            src_ref=dst, dst_ref=dst,
            send_sem=send_sem.at[0], recv_sem=recv_sem.at[slot], device_id=to,
        ).wait_recv()

    def drain(n=None):
        for copy in sent[:n]:
            copy.wait_send()
        waited.extend(sent[:n])
        del sent[:n]

    def exchange(others, me, to, source, target, n):
        slot = take(n)
        for q in others:
            send(source(q), target(me), slot + me, to(q))

        def finish():
            for q in others:
                receive(target(q), slot + q, to(q))

        return finish

    for copy in loads[:3]:
        copy.wait()
    stream = stream_ref[...].astype(F32)
    scaled = (stream * gain_ref[...]).astype(BF16)
    squares = jnp.sum(stream * stream, axis=1, keepdims=True)
    lane = lax.broadcasted_iota(jnp.int32, (mine, LANES), 1)
    norm_parts[x] = scaled[:, 0:head]
    extra_parts[dep, :, 0:wide] = mixed_ref[...]
    extra_parts[dep, :, wide:end] = scaled[:, head:wide]
    rounded = squares.astype(BF16).astype(F32)
    first = spare - last + 2 * core
    rest = jnp.where(lane == first + 1, squares - rounded, 0.0)
    extra_parts[dep, :, end : end + LANES] = jnp.where(lane == first, rounded, rest).astype(BF16)

    pl.semaphore_wait(barrier, len(peers))
    n1 = exchange(x_peers, x, to_x, lambda q: norm_parts.at[x], lambda q: norm_parts.at[q], X)
    d1 = exchange(depths, dep, to_depth, lambda q: extra_parts.at[dep], lambda q: extra_parts.at[q], Y)
    n1()
    norm_all[plane, dep] = norm_parts[...].astype(F32).reshape(norm_all.shape[2:]).astype(BF16)
    over = take(2)
    ours = norm_all.at[plane, dep]
    send(ours, ours, over, to_plane)

    def spread_norm(p):
        return exchange(depths, dep, to_depth, lambda q: norm_all.at[p, dep], lambda q: norm_all.at[p, q], Y)

    def spread_extra(p):
        return exchange(x_peers, x, to_x, lambda q: extra_rows.at[p, x], lambda q: extra_rows.at[p, q], X)

    n2 = [spread_norm(plane)]
    d1()
    extra_rows[plane, x] = extra_parts[...].astype(F32).reshape(extra_rows.shape[2:]).astype(BF16)
    ours = extra_rows.at[plane, x]
    send(ours, ours, over + 1, to_plane)
    d2 = [spread_extra(plane)]

    for copy in loads[3:]:
        copy.wait()
    w_down[fh:high, :] = jnp.zeros((high - fh, wide), BF16)
    w_both[low:fh, :] = jnp.zeros((fh - low, wide), BF16)
    w_both[spare:fw, :] = jnp.zeros((fw - spare, wide), BF16)
    wt_both[...] = jnp.transpose(w_both[low:fw, :])
    wt_down[...] = jnp.transpose(w_down[...])
    t = lax.broadcasted_iota(jnp.int32, (half, half), 0)
    u = lax.broadcasted_iota(jnp.int32, (half, half), 1)
    there = ((t // mine) % X) * (Y * mine) + (t // (X * mine)) * mine + t % mine
    by_depth = (u == there).astype(F32).astype(BF16)
    there = ((t // mine) % Y) * (X * mine) + (t // (Y * mine)) * mine + t % mine
    by_x = (u == there).astype(F32).astype(BF16)

    drain(-3)
    receive(norm_all.at[1 - plane, dep], over, to_plane)
    n2.append(spread_norm(1 - plane))
    receive(extra_rows.at[1 - plane, x], over + 1, to_plane)
    d2.append(spread_extra(1 - plane))

    quad = []
    for h, p in enumerate(planes):
        d2[h]()
        extra = dot(by_depth, extra_rows[p].reshape(half, end + LANES)).astype(BF16)
        extra_all[p] = extra
        both = dot(extra[:, wide:end], wt_both[head:wide, :])
        dh = dot(extra[:, 0:wide], wt_down[...]).reshape(2, Z, X * mine, high)
        partial[p, :, :, :, 0:low] = dh[:, :, :, 0:low]
        n2[h]()
        both += dot(norm_all[p].reshape(half, head), wt_both[0:head, :])
        both = both.reshape(2, Z, X * mine, fw - low)
        partial[p, :, :, :, low:fw] = both
        partial[p, :, :, :, last:fw] += extra[:, end : end + LANES].astype(F32).reshape(2, Z, X * mine, LANES)
        partial[p, :, :, :, low:high] += dh[:, :, :, low:high]
        pair = take(1)
        send(partial.at[p, 1 - core], pair_in.at[p], pair, to_core)
        receive(pair_in.at[p], pair, to_core)
        for q in others:
            quad_out[p, q] = (partial[p, core, q] + pair_in[p, q]).astype(BF16)
        quad.append(exchange(others, zh, to_chip, lambda q: quad_out.at[p, q], lambda q, p=p: quad_in.at[p, q], Z))

    share = []
    for h, p in enumerate(planes):
        quad[h]()
        total = partial[p, core, zh] + pair_in[p, zh]
        for q in others:
            total = total + quad_in[p, q].astype(F32)
        squares = sum(total[:, spare + i : spare + i + 1] for i in range(4))
        inv = lax.rsqrt(squares / D + EPSILON)
        dh = total[:, 0:fh]
        gate = inv * total[:, fh : 2 * fh]
        up = inv * total[:, 2 * fh : 3 * fh]
        sigma = jax.nn.sigmoid(gate)
        act = gate * sigma
        d_gate = dh * up * sigma * (1.0 + gate * (1.0 - sigma))
        d_up = dh * act
        inner = inv * inv * jnp.sum(d_gate * gate + d_up * up, axis=1, keepdims=True)
        lane = lax.broadcasted_iota(jnp.int32, (total.shape[0], LANES), 1)
        act_all[p, core, zh, :, last:fw] = jnp.where(lane == spare - last, inner, 0.0).astype(BF16)
        act_all[p, core, zh, :, 0:fh] = (act * up).astype(BF16)
        act_all[p, core, zh, :, fh : 2 * fh] = (inv * d_gate).astype(BF16)
        act_all[p, core, zh, :, 2 * fh : 3 * fh] = (inv * d_up).astype(BF16)
        share.append(exchange(others, zh, to_chip, lambda q: act_all.at[p, core, zh], lambda q, p=p: act_all.at[p, core, q], Z))

    e1, o1 = [], []
    for h, p in enumerate(planes):
        side = take(1)
        share[h]()
        send(act_all.at[p, core], act_all.at[p, core], side, to_core)
        receive(act_all.at[p, 1 - core], side, to_core)
        acts = act_all[p].reshape(half, fw)
        out_send[p] = dot(acts[:, 0:high], w_down[:, 0:head]).astype(BF16).reshape(Y, X * mine, head)
        o1.append(exchange(depths, dep, to_depth, lambda q: out_send.at[p, q], lambda q, p=p: out_recv.at[p, q], Y))
        acts = dot(by_x, acts).astype(BF16)
        dn_send[p, :, :, 0:wide] = dot(acts[:, low:fw], w_both[low:fw, :]).astype(BF16).reshape(X, Y * mine, wide)
        dn_send[p, :, :, wide:end] = dot(acts[:, 0:high], w_down[:, head:wide]).astype(BF16).reshape(X, Y * mine, wide - head)
        dn_send[p, :, :, end : end + LANES] = acts[:, last:fw].reshape(X, Y * mine, LANES)
        e1.append(exchange(x_peers, x, to_x, lambda q: dn_send.at[p, q], lambda q, p=p: dn_recv.at[p, q], X))
        out_recv[p, dep] = out_send[p, dep]
        dn_recv[p, x] = dn_send[p, x]

    drain(-(len(depths) + len(x_peers)))

    flipped = jnp.transpose(act_all[...].reshape(2 * half, fw))
    extra = extra_all[...].reshape(2 * half, end + LANES)
    normed = norm_all[...].reshape(2 * half, head)
    gd_out[...] = dot(flipped[0:fh], extra[:, 0:wide]).astype(BF16)
    for i, out in ((1, gg_out), (2, gu_out)):
        out[:, 0:head] = dot(flipped[i * fh : (i + 1) * fh], normed).astype(BF16)
        out[:, head:wide] = dot(flipped[i * fh : (i + 1) * fh], extra[:, wide:end]).astype(BF16)

    def add(ref, n):
        total = ref[0].astype(F32)
        for q in range(1, n):
            total = total + ref[q].astype(F32)
        return total

    def split(total, ref, n):
        for q in range(n):
            ref[q] = total[q * mine : (q + 1) * mine].astype(BF16)

    e2, o2 = take(2 * Y), take(2 * X)
    for h, p in enumerate(planes):
        e1[h]()
        split(add(dn_recv.at[p], X), dn_send2.at[p], Y)
        for q in depths if h == 0 else [*depths, dep]:
            to = {"depth": q} if h == 0 else {"row": across + x, "depth": q}
            send(dn_send2.at[p, q], dn_recv2.at[plane, dep], e2 + plane * Y + dep, to)
        o1[h]()
        split(add(out_recv.at[p], Y), out_send2.at[p], X)
        for q in x_peers if h == 0 else [*x_peers, x]:
            send(out_send2.at[p, q], out_recv2.at[plane, x], o2 + plane * X + x, {"row": p * X + q})
    out_recv2[plane, x] = out_send2[plane, x]
    dn_recv2[plane, dep] = dn_send2[plane, dep]

    for h, p in enumerate(planes):
        for q in x_peers if h == 0 else [*x_peers, x]:
            receive(out_recv2.at[p, q], o2 + p * X + q, {"row": p * X + q})
    total = add(out_recv2.at[0], X) + add(out_recv2.at[1], X)
    new_out[:, 0:head] = (stream[:, 0:head] + total).astype(BF16)
    for h, p in enumerate(planes):
        for q in depths if h == 0 else [*depths, dep]:
            to = {"depth": q} if h == 0 else {"row": across + x, "depth": q}
            receive(dn_recv2.at[p, q], e2 + p * Y + q, to)
    total = add(dn_recv2.at[0], Y) + add(dn_recv2.at[1], Y)
    inner = total[:, end + spare - last : end + spare - last + 1]
    dstream_out[...] = (
        mixed_ref[...].astype(F32) + gain_ref[...] * total[:, 0:wide] - stream * (inner / D)
    ).astype(BF16)
    new_out[:, head:wide] = (stream[:, head:wide] + total[:, wide:end]).astype(BF16)

    drain()


def hand_over(*refs):
    n = len(refs) // 2
    copies = [pltpu.make_async_copy(refs[i], refs[n + i], refs[2 * n].at[i]) for i in range(n)]
    for copy in copies:
        copy.start()
    for copy in copies:
        copy.wait()


def on_device(axes, stream, norm_gain, w_gate, w_up, w_down, d_mixed):
    R, C, Y = axes
    mine, wide = stream.shape
    fh = w_gate.shape[1]
    fw = (3 * fh // LANES + 1) * LANES
    low, high = fh // LANES * LANES, pl.cdiv(fh, LANES) * LANES
    head = wide // LANES * 3 // 4 * LANES
    both = 2 * wide - head + LANES
    Z, X = C // 2, R // 2
    assert Y == C
    half = X * Y * mine
    vmem = lambda *shape: pltpu.VMEM(shape, BF16)
    f32 = lambda *shape: pltpu.VMEM(shape, F32)
    near = pl.BlockSpec(memory_space=pltpu.VMEM)
    far = pl.BlockSpec(memory_space=pltpu.HBM)
    shape = lambda *a: jax.ShapeDtypeStruct(a, BF16)
    shapes = (shape(mine, wide),) * 2 + (shape(fh, wide),) * 3
    outs = pl.pallas_call(
        functools.partial(kernel, (R, C, Y, fh, wide * C)),
        out_shape=tuple(pltpu.VMEM(a.shape, BF16) for a in shapes),
        in_specs=[far] * 6,
        out_specs=[near] * 5,
        scratch_shapes=[
            vmem(mine, wide), vmem(mine, wide), f32(1, wide),
            vmem(high, wide), vmem(fw, wide), vmem(wide, high), vmem(wide, fw - low),
            vmem(X, mine, head), vmem(2, Y, X * mine, head),
            vmem(Y, mine, both), vmem(2, X, Y * mine, both), vmem(2, half, both),
            f32(2, 2, Z, X * mine, fw), f32(2, Z, X * mine, fw),
            vmem(2, Z, X * mine, fw), vmem(2, Z, X * mine, fw),
            vmem(2, 2, Z, X * mine, fw),
            vmem(2, Y, X * mine, head), vmem(2, Y, X * mine, head), vmem(2, X, mine, head), vmem(2, X, mine, head),
            vmem(2, X, Y * mine, both), vmem(2, X, Y * mine, both), vmem(2, Y, mine, both), vmem(2, Y, mine, both),
            pltpu.SemaphoreType.DMA((6,)),
            pltpu.SemaphoreType.DMA((160,)),
            pltpu.SemaphoreType.DMA((160,)),
        ],
        compiler_params=pltpu.CompilerParams(
            collective_id=0, has_side_effects=True, vmem_limit_bytes=61 << 20
        ),
    )(stream, d_mixed, norm_gain.reshape(1, wide), w_gate.T, w_up.T, w_down)
    new, dstream, gg, gu, gd = pl.pallas_call(
        hand_over,
        out_shape=shapes,
        in_specs=[near] * 5,
        out_specs=[far] * 5,
        scratch_shapes=[pltpu.SemaphoreType.DMA((5,))],
        compiler_params=pltpu.CompilerParams(vmem_limit_bytes=1 << 20),
    )(*outs)
    return new, dstream, gg.T, gu.T, gd


def solution(mesh):
    tokens, weights = P(("row", "depth"), "col"), P("col", ("row", "depth"))
    return jax.shard_map(
        functools.partial(on_device, tuple(mesh.shape[a] for a in ("row", "col", "depth"))),
        mesh=mesh,
        in_specs=(tokens, P("col"), weights, weights, tokens, tokens),
        out_specs=(tokens, tokens, weights, weights, tokens),
        check_vma=False,
    )
```

```python
import functools

import jax
import jax.numpy as jnp
from jax import lax
from jax.experimental import pallas as pl
from jax.experimental.pallas import tpu as pltpu
from jax.sharding import PartitionSpec as P

F32, BF16 = jnp.float32, jnp.bfloat16
LANES = 128
EPSILON = 1e-05


def dot(a, b, dims=((1,), (0,))):
    return lax.dot_general(a, b, (dims, ((), ())), preferred_element_type=F32)


def kernel(
    sizes,
    stream_hbm, mixed_hbm, gain_hbm, wg_hbm, wu_hbm, wd_hbm,
    new_out, dstream_out, gg_out, gu_out, gd_out,
    stream_ref, mixed_ref, gain_ref, w_down, w_both, wt_down, wt_both,
    norm_parts, norm_all, extra_parts, extra_rows, extra_all,
    partial, pair_in, quad_out, quad_in,
    act_all,
    out_send, out_recv, out_send2, out_recv2,
    dn_send, dn_recv, dn_send2, dn_recv2,
    local_sem, send_sem, recv_sem,
):
    R, C, Y, fh, D = sizes
    mine, wide = stream_ref.shape
    head = norm_all.shape[3]
    fw = act_all.shape[4]
    low, high = fh // LANES * LANES, pl.cdiv(fh, LANES) * LANES
    spare = 3 * fh
    last = fw - LANES
    end = 2 * wide - head
    Z, X = C // 2, R // 2
    half = X * Y * mine
    row, col, dep = (lax.axis_index(a) for a in ("row", "col", "depth"))
    zh, core = lax.div(col, 2), lax.rem(col, 2)
    plane, x = lax.div(row, X), lax.rem(row, X)
    planes = (plane, 1 - plane)
    loads = [
        pltpu.make_async_copy(a, b, local_sem.at[i])
        for i, (a, b) in enumerate([
            (stream_hbm, stream_ref),
            (gain_hbm, gain_ref),
            (mixed_hbm, mixed_ref),
            (wg_hbm, w_both.at[pl.ds(fh, fh)]),
            (wu_hbm, w_both.at[pl.ds(2 * fh, fh)]),
            (wd_hbm, w_down.at[pl.ds(0, fh)]),
        ])
    ]
    for copy in loads[:3]:
        copy.start()

    far = lambda n: sorted(range(1, n), key=lambda k: abs(k - n // 2))
    x_peers = [lax.rem(x + k, X) for k in far(X)]
    depths = [lax.rem(dep + k, Y) for k in far(Y)]
    others = [lax.rem(zh + k, Z) for k in far(Z)]
    across = (1 - plane) * X
    to_x = lambda q: {"row": plane * X + q}
    to_depth = lambda q: {"depth": q}
    to_plane = {"row": across + x}
    to_chip = lambda q: {"col": q * 2 + core}
    to_core = {"col": zh * 2 + 1 - core}
    peers = [to_plane, to_core]
    peers += [to_x(q) for q in x_peers] + [{"row": across + q} for q in x_peers]
    peers += [to_chip(q) for q in others] + [to_depth(q) for q in depths]
    peers += [{"row": across + x, "depth": q} for q in depths]
    barrier = pltpu.get_barrier_semaphore()
    for peer in reversed(peers):
        pl.semaphore_signal(barrier, 1, device_id=peer)
    for copy in loads[3:]:
        copy.start()

    sent, slots, waited = [], iter(range(160)), []

    def take(n):
        return [next(slots) for _ in range(n)][0]

    def send(src, dst, slot, to):
        copy = pltpu.make_async_remote_copy(
            src_ref=src, dst_ref=dst,
            send_sem=send_sem.at[len(waited) + len(sent)], recv_sem=recv_sem.at[slot], device_id=to,
        )
        copy.start()
        sent.append(copy)

    def receive(dst, slot, to):
        pltpu.make_async_remote_copy(
            src_ref=dst, dst_ref=dst,
            send_sem=send_sem.at[0], recv_sem=recv_sem.at[slot], device_id=to,
        ).wait_recv()

    def drain(n=None):
        for copy in sent[:n]:
            copy.wait_send()
        waited.extend(sent[:n])
        del sent[:n]

    def exchange(others, me, to, source, target, n):
        slot = take(n)
        for q in others:
            send(source(q), target(me), slot + me, to(q))

        def finish(only=others):
            for q in only:
                receive(target(q), slot + q, to(q))

        return finish

    for copy in loads[:3]:
        copy.wait()
    stream = stream_ref[...].astype(F32)
    scaled = (stream * gain_ref[...]).astype(BF16)
    squares = jnp.sum(stream * stream, axis=1, keepdims=True)
    lane = lax.broadcasted_iota(jnp.int32, (mine, LANES), 1)
    norm_parts[x] = scaled[:, 0:head]
    extra_parts[dep, :, 0:wide] = mixed_ref[...]
    extra_parts[dep, :, wide:end] = scaled[:, head:wide]
    rounded = squares.astype(BF16).astype(F32)
    first = spare - last + 2 * core
    rest = jnp.where(lane == first + 1, squares - rounded, 0.0)
    extra_parts[dep, :, end : end + LANES] = jnp.where(lane == first, rounded, rest).astype(BF16)

    pl.semaphore_wait(barrier, len(peers))
    n1 = exchange(x_peers, x, to_x, lambda q: norm_parts.at[x], lambda q: norm_parts.at[q], X)
    d1 = exchange(depths, dep, to_depth, lambda q: extra_parts.at[dep], lambda q: extra_parts.at[q], Y)
    n1()
    norm_all[plane, dep] = norm_parts[...].astype(F32).reshape(norm_all.shape[2:]).astype(BF16)
    over = take(2)
    ours = norm_all.at[plane, dep]
    send(ours, ours, over, to_plane)

    def spread_norm(p):
        return exchange(depths, dep, to_depth, lambda q: norm_all.at[p, dep], lambda q: norm_all.at[p, q], Y)

    def spread_extra(p):
        return exchange(x_peers, x, to_x, lambda q: extra_rows.at[p, x], lambda q: extra_rows.at[p, q], X)

    n2 = [spread_norm(plane)]
    d1()
    extra_rows[plane, x] = extra_parts[...].astype(F32).reshape(extra_rows.shape[2:]).astype(BF16)
    ours = extra_rows.at[plane, x]
    send(ours, ours, over + 1, to_plane)
    d2 = [spread_extra(plane)]

    for copy in loads[3:]:
        copy.wait()
    w_down[fh:high, :] = jnp.zeros((high - fh, wide), BF16)
    w_both[low:fh, :] = jnp.zeros((fh - low, wide), BF16)
    w_both[spare:fw, :] = jnp.zeros((fw - spare, wide), BF16)
    wt_both[...] = jnp.transpose(w_both[low:fw, :])
    wt_down[...] = jnp.transpose(w_down[...])
    t = lax.broadcasted_iota(jnp.int32, (half, half), 0)
    u = lax.broadcasted_iota(jnp.int32, (half, half), 1)
    there = ((t // mine) % X) * (Y * mine) + (t // (X * mine)) * mine + t % mine
    by_depth = (u == there).astype(F32).astype(BF16)
    there = ((t // mine) % Y) * (X * mine) + (t // (Y * mine)) * mine + t % mine
    by_x = (u == there).astype(F32).astype(BF16)

    drain(-3)
    receive(norm_all.at[1 - plane, dep], over, to_plane)
    n2.append(spread_norm(1 - plane))
    receive(extra_rows.at[1 - plane, x], over + 1, to_plane)
    d2.append(spread_extra(1 - plane))

    quad = []
    for h, p in enumerate(planes):
        d2[h]()
        extra = dot(by_depth, extra_rows[p].reshape(half, end + LANES)).astype(BF16)
        extra_all[p] = extra
        both = dot(extra[:, wide:end], wt_both[head:wide, :])
        dh = dot(extra[:, 0:wide], wt_down[...]).reshape(2, Z, X * mine, high)
        partial[p, :, :, :, 0:low] = dh[:, :, :, 0:low]
        n2[h]()
        both += dot(norm_all[p].reshape(half, head), wt_both[0:head, :])
        both = both.reshape(2, Z, X * mine, fw - low)
        partial[p, :, :, :, low:fw] = both
        partial[p, :, :, :, last:fw] += extra[:, end : end + LANES].astype(F32).reshape(2, Z, X * mine, LANES)
        partial[p, :, :, :, low:high] += dh[:, :, :, low:high]
        pair = take(1)
        send(partial.at[p, 1 - core], pair_in.at[p], pair, to_core)
        receive(pair_in.at[p], pair, to_core)
        for q in others:
            quad_out[p, q] = (partial[p, core, q] + pair_in[p, q]).astype(BF16)
        quad.append(exchange(others, zh, to_chip, lambda q: quad_out.at[p, q], lambda q, p=p: quad_in.at[p, q], Z))

    share = []
    for h, p in enumerate(planes):
        quad[h]()
        total = partial[p, core, zh] + pair_in[p, zh]
        for q in others:
            total = total + quad_in[p, q].astype(F32)
        squares = sum(total[:, spare + i : spare + i + 1] for i in range(4))
        inv = lax.rsqrt(squares / D + EPSILON)
        dh = total[:, 0:fh]
        gate = inv * total[:, fh : 2 * fh]
        up = inv * total[:, 2 * fh : 3 * fh]
        sigma = jax.nn.sigmoid(gate)
        act = gate * sigma
        d_gate = dh * up * sigma * (1.0 + gate * (1.0 - sigma))
        d_up = dh * act
        inner = inv * inv * jnp.sum(d_gate * gate + d_up * up, axis=1, keepdims=True)
        lane = lax.broadcasted_iota(jnp.int32, (total.shape[0], LANES), 1)
        act_all[p, core, zh, :, last:fw] = jnp.where(lane == spare - last, inner, 0.0).astype(BF16)
        act_all[p, core, zh, :, 0:fh] = (act * up).astype(BF16)
        act_all[p, core, zh, :, fh : 2 * fh] = (inv * d_gate).astype(BF16)
        act_all[p, core, zh, :, 2 * fh : 3 * fh] = (inv * d_up).astype(BF16)
        share.append(exchange(others, zh, to_chip, lambda q: act_all.at[p, core, zh], lambda q, p=p: act_all.at[p, core, q], Z))

    e1, o1 = [], []
    for h, p in enumerate(planes):
        side = take(Z)
        for q in [zh, *others[1:], others[0]]:
            if q is not zh:
                share[h]([q])
            ours = act_all.at[p, core, q]
            send(ours, ours, side + q, to_core)
        for q in [zh, *others]:
            receive(act_all.at[p, 1 - core, q], side + q, to_core)
        acts = act_all[p].reshape(half, fw)
        out_send[p] = dot(acts[:, 0:high], w_down[:, 0:head]).astype(BF16).reshape(Y, X * mine, head)
        o1.append(exchange(depths, dep, to_depth, lambda q: out_send.at[p, q], lambda q, p=p: out_recv.at[p, q], Y))
        acts = dot(by_x, acts).astype(BF16)
        dn_send[p, :, :, 0:wide] = dot(acts[:, low:fw], w_both[low:fw, :]).astype(BF16).reshape(X, Y * mine, wide)
        dn_send[p, :, :, wide:end] = dot(acts[:, 0:high], w_down[:, head:wide]).astype(BF16).reshape(X, Y * mine, wide - head)
        dn_send[p, :, :, end : end + LANES] = acts[:, last:fw].reshape(X, Y * mine, LANES)
        e1.append(exchange(x_peers, x, to_x, lambda q: dn_send.at[p, q], lambda q, p=p: dn_recv.at[p, q], X))
        out_recv[p, dep] = out_send[p, dep]
        dn_recv[p, x] = dn_send[p, x]

    drain(-(len(depths) + len(x_peers)))

    flipped = jnp.transpose(act_all[...].reshape(2 * half, fw))
    extra = extra_all[...].reshape(2 * half, end + LANES)
    normed = norm_all[...].reshape(2 * half, head)
    gd_out[...] = dot(flipped[0:fh], extra[:, 0:wide]).astype(BF16)
    for i, out in ((1, gg_out), (2, gu_out)):
        out[:, 0:head] = dot(flipped[i * fh : (i + 1) * fh], normed).astype(BF16)
        out[:, head:wide] = dot(flipped[i * fh : (i + 1) * fh], extra[:, wide:end]).astype(BF16)

    def add(ref, n):
        total = ref[0].astype(F32)
        for q in range(1, n):
            total = total + ref[q].astype(F32)
        return total

    def split(total, ref, n):
        for q in range(n):
            ref[q] = total[q * mine : (q + 1) * mine].astype(BF16)

    e2, o2 = take(2 * Y), take(2 * X)
    for h, p in enumerate(planes):
        e1[h]()
        split(add(dn_recv.at[p], X), dn_send2.at[p], Y)
        for q in depths if h == 0 else [*depths, dep]:
            to = {"depth": q} if h == 0 else {"row": across + x, "depth": q}
            send(dn_send2.at[p, q], dn_recv2.at[plane, dep], e2 + plane * Y + dep, to)
        o1[h]()
        split(add(out_recv.at[p], Y), out_send2.at[p], X)
        for q in x_peers if h == 0 else [*x_peers, x]:
            send(out_send2.at[p, q], out_recv2.at[plane, x], o2 + plane * X + x, {"row": p * X + q})
    out_recv2[plane, x] = out_send2[plane, x]
    dn_recv2[plane, dep] = dn_send2[plane, dep]

    for h, p in enumerate(planes):
        for q in x_peers if h == 0 else [*x_peers, x]:
            receive(out_recv2.at[p, q], o2 + p * X + q, {"row": p * X + q})
    total = add(out_recv2.at[0], X) + add(out_recv2.at[1], X)
    new_out[:, 0:head] = (stream[:, 0:head] + total).astype(BF16)
    for h, p in enumerate(planes):
        for q in depths if h == 0 else [*depths, dep]:
            to = {"depth": q} if h == 0 else {"row": across + x, "depth": q}
            receive(dn_recv2.at[p, q], e2 + p * Y + q, to)
    total = add(dn_recv2.at[0], Y) + add(dn_recv2.at[1], Y)
    inner = total[:, end + spare - last : end + spare - last + 1]
    dstream_out[...] = (
        mixed_ref[...].astype(F32) + gain_ref[...] * total[:, 0:wide] - stream * (inner / D)
    ).astype(BF16)
    new_out[:, head:wide] = (stream[:, head:wide] + total[:, wide:end]).astype(BF16)

    drain()


def hand_over(*refs):
    n = len(refs) // 2
    copies = [pltpu.make_async_copy(refs[i], refs[n + i], refs[2 * n].at[i]) for i in range(n)]
    for copy in copies:
        copy.start()
    for copy in copies:
        copy.wait()


def on_device(axes, stream, norm_gain, w_gate, w_up, w_down, d_mixed):
    R, C, Y = axes
    mine, wide = stream.shape
    fh = w_gate.shape[1]
    fw = (3 * fh // LANES + 1) * LANES
    low, high = fh // LANES * LANES, pl.cdiv(fh, LANES) * LANES
    head = wide // LANES * 3 // 4 * LANES
    both = 2 * wide - head + LANES
    Z, X = C // 2, R // 2
    assert Y == C
    half = X * Y * mine
    vmem = lambda *shape: pltpu.VMEM(shape, BF16)
    f32 = lambda *shape: pltpu.VMEM(shape, F32)
    near = pl.BlockSpec(memory_space=pltpu.VMEM)
    far = pl.BlockSpec(memory_space=pltpu.HBM)
    shape = lambda *a: jax.ShapeDtypeStruct(a, BF16)
    shapes = (shape(mine, wide),) * 2 + (shape(fh, wide),) * 3
    outs = pl.pallas_call(
        functools.partial(kernel, (R, C, Y, fh, wide * C)),
        out_shape=tuple(pltpu.VMEM(a.shape, BF16) for a in shapes),
        in_specs=[far] * 6,
        out_specs=[near] * 5,
        scratch_shapes=[
            vmem(mine, wide), vmem(mine, wide), f32(1, wide),
            vmem(high, wide), vmem(fw, wide), vmem(wide, high), vmem(wide, fw - low),
            vmem(X, mine, head), vmem(2, Y, X * mine, head),
            vmem(Y, mine, both), vmem(2, X, Y * mine, both), vmem(2, half, both),
            f32(2, 2, Z, X * mine, fw), f32(2, Z, X * mine, fw),
            vmem(2, Z, X * mine, fw), vmem(2, Z, X * mine, fw),
            vmem(2, 2, Z, X * mine, fw),
            vmem(2, Y, X * mine, head), vmem(2, Y, X * mine, head), vmem(2, X, mine, head), vmem(2, X, mine, head),
            vmem(2, X, Y * mine, both), vmem(2, X, Y * mine, both), vmem(2, Y, mine, both), vmem(2, Y, mine, both),
            pltpu.SemaphoreType.DMA((6,)),
            pltpu.SemaphoreType.DMA((160,)),
            pltpu.SemaphoreType.DMA((160,)),
        ],
        compiler_params=pltpu.CompilerParams(
            collective_id=0, has_side_effects=True, vmem_limit_bytes=61 << 20
        ),
    )(stream, d_mixed, norm_gain.reshape(1, wide), w_gate.T, w_up.T, w_down)
    new, dstream, gg, gu, gd = pl.pallas_call(
        hand_over,
        out_shape=shapes,
        in_specs=[near] * 5,
        out_specs=[far] * 5,
        scratch_shapes=[pltpu.SemaphoreType.DMA((5,))],
        compiler_params=pltpu.CompilerParams(vmem_limit_bytes=1 << 20),
    )(*outs)
    return new, dstream, gg.T, gu.T, gd


def solution(mesh):
    tokens, weights = P(("row", "depth"), "col"), P("col", ("row", "depth"))
    return jax.shard_map(
        functools.partial(on_device, tuple(mesh.shape[a] for a in ("row", "col", "depth"))),
        mesh=mesh,
        in_specs=(tokens, P("col"), weights, weights, tokens, tokens),
        out_specs=(tokens, tokens, weights, weights, tokens),
        check_vma=False,
    )
```
